32 devices in a mesh: dp: 4 (over y, x), mp: 8 (over z, core).
Axes of the slice: x: 2, y: 2, z: 4, core: 2. Of those that a mesh axis runs over, the one named last changes fastest.
Arguments:
- hidden_states: bfloat16 [2048, 4096], P('dp', 'mp'), may hold values from -6 to 6
- gate_online: bfloat16 [4096, 14336], P('dp', 'mp'), may hold values from -0.09375 to 0.09375
- up_online: bfloat16 [4096, 14336], P('dp', 'mp'), may hold values from -0.09375 to 0.09375
- down_online: bfloat16 [14336, 4096], P('mp', 'dp'), may hold values from -0.046875 to 0.046875
- gate_previous: bfloat16 [4096, 14336], P(None, 'mp'), may hold values from -0.09375 to 0.09375
- up_previous: bfloat16 [4096, 14336], P(None, 'mp'), may hold values from -0.09375 to 0.09375
- down_previous: bfloat16 [14336, 4096], P('mp'), may hold values from -0.046875 to 0.046875
Outputs:
- online_output: bfloat16 [2048, 4096], P('dp', 'mp')
- target_output: bfloat16 [2048, 4096], P('dp', 'mp')
The draws below stay inside these ranges and needn't reach their ends.
All inputs are finite; a program needn't handle non-finite values.
Results may differ from the reference program's by a relative error of at most 0.0072.
Values may be sent and summed in bfloat16 or wider, within the bound.
No kernel may reach another device: no remote copies, remote signals or barrier semaphores. Data moves between devices by JAX's collectives and lax.ppermute only.
A program may use at most 192 MiB of HBM per device.

```python
import jax
import jax.numpy as jnp

D = 4096
FF = 14336
TOKENS = 2048


def levels(rng, shape, split, least, largest):
    def one(dim, blocks):
        steps = jax.random.uniform(jax.random.fold_in(jax.random.fold_in(rng, 6), dim), (blocks,), jnp.float32, least / len(split), largest / len(split))
        return jnp.repeat(jnp.exp(steps), shape[dim] // blocks).reshape((-1,) + (1,) * (len(shape) - dim - 1))

    loudness = one(*split[0])
    for cut in split[1:]:
        loudness = loudness * one(*cut)
    return loudness


def scatter_about(own_key, extent, width, limit, split=(), kind=jnp.bfloat16):
    values = jax.random.normal(own_key, extent, jnp.float32) * width
    if len(split) > 0:
        values = levels(own_key, extent, split, -0.22, 0.18) * values
    return jnp.clip(values, min=-limit, max=limit).astype(kind)


def setup_inputs(seed: int = 0) -> dict:
    splits = jax.random.split(jax.random.key(seed), 8)
    hidden_states = scatter_about(splits[0], (TOKENS, D), 1.0, 6.0, ((0, 4), (1, 8)))
    gate_online = scatter_about(splits[1], (D, FF), D ** -0.5, 0.09375, ((0, 4), (1, 8)))
    up_online = scatter_about(splits[2], (D, FF), D ** -0.5, 0.09375, ((0, 4), (1, 8)))
    down_online = scatter_about(splits[3], (FF, D), FF ** -0.5, 0.046875, ((0, 8), (1, 4)))
    gate_previous = scatter_about(splits[4], (D, FF), D ** -0.5, 0.09375, ((1, 8),))
    up_previous = scatter_about(splits[5], (D, FF), D ** -0.5, 0.09375, ((1, 8),))
    down_previous = scatter_about(splits[6], (FF, D), FF ** -0.5, 0.046875, ((0, 8),))
    return {"hidden_states": hidden_states, "gate_online": gate_online, "up_online": up_online, "down_online": down_online, "gate_previous": gate_previous, "up_previous": up_previous, "down_previous": down_previous}


POLYAK = 0.25


def blend(online, previous):
    return (POLYAK * online.astype(jnp.float32) + (1.0 - POLYAK) * previous.astype(jnp.float32)).astype(jnp.bfloat16)


def forward(inputs, gate_weight, up_weight, down_weight):
    gate = jnp.dot(inputs, gate_weight, preferred_element_type=jnp.float32)
    up_part = jnp.dot(inputs, up_weight, preferred_element_type=jnp.float32)
    inner = (jax.nn.silu(gate) * up_part).astype(jnp.bfloat16)
    return jnp.dot(inner, down_weight, preferred_element_type=jnp.float32).astype(jnp.bfloat16)


def reference(hidden_states, gate_online, up_online, down_online, gate_previous, up_previous, down_previous):
    online_output = forward(hidden_states, gate_online, up_online, down_online)
    target_output = forward(hidden_states, blend(gate_online, gate_previous), blend(up_online, up_previous), blend(down_online, down_previous))
    return online_output, target_output
```

```python
import functools

import jax
import jax.numpy as jnp
from jax import lax
from jax.experimental import pallas as pl
from jax.experimental.pallas import tpu as pltpu
from jax.sharding import PartitionSpec as P

POLYAK = 0.25
TILE = 1024
VMEM_BYTES = 56 * 1024 * 1024
CHEAP = pl.CostEstimate(flops=1, bytes_accessed=1, transcendentals=0)


def blend(online, previous):
    return (
        POLYAK * online.astype(jnp.float32) + (1.0 - POLYAK) * previous.astype(jnp.float32)
    ).astype(jnp.bfloat16)


def dot(a, b):
    return jnp.dot(a, b, preferred_element_type=jnp.float32)


def silu(v):
    return v / (1.0 + jnp.exp(-v))


def hidden_kernel(n, n_start, n_gates, n_after, order, *refs):
    refs = list(refs)

    def take(count):
        out = refs[:count]
        del refs[:count]
        return out

    (features,) = take(1)
    online, (previous,) = take(n), take(1)
    more = take(n_start + n_gates)
    take(n_after)
    outs = take(2)
    f_buf, on_buf, old_buf = take(3)
    more_buf = take(len(more))
    acc = take(2)
    target, sems = take(2)
    rows, units = on_buf.shape[1:]
    tokens = f_buf.shape[1]
    copies = []
    for k in range(n):
        at = pl.ds(pl.multiple_of(order[k] * rows, rows), rows)
        old = previous.at[at]
        if previous.shape[1] != units:
            old = old.at[:, pl.ds(pl.multiple_of(order[n], 128), units)]
        group = [
            pltpu.make_async_copy(online[k], on_buf.at[k], sems.at[3 * k]),
            pltpu.make_async_copy(old, old_buf.at[k], sems.at[3 * k + 1]),
            pltpu.make_async_copy(features.at[:, at], f_buf.at[k], sems.at[3 * k + 2]),
        ]
        for copy in group:
            copy.start()
        copies.append(group)
    last = [
        pltpu.make_async_copy(src, dst, sems.at[3 * n + m])
        for m, (src, dst) in enumerate(zip(more, more_buf))
    ]
    for copy in last:
        copy.start()
    tile = min(TILE, tokens)
    starts = more_buf[:n_start]
    gates = more_buf[n_start:]
    for k in range(n):
        for copy in copies[k]:
            copy.wait()
        target[...] = blend(on_buf[k], old_buf[k])
        if k == n - 1:
            for copy in last:
                copy.wait()

        @pl.loop(0, tokens // tile)
        def _(t):
            here = pl.ds(pl.multiple_of(t * tile, tile), tile)
            f = f_buf[k, here, :]
            for m, w in enumerate((on_buf.at[k], target)):
                s = dot(f, w[...])
                if k > 0:
                    s = s + acc[m][here, :]
                if k == n - 1:
                    if starts:
                        s = s + starts[m][here, :]
                    if gates:
                        s = silu(gates[m][here, :]) * s
                    outs[m][here, :] = s.astype(outs[m].dtype)
                else:
                    acc[m][here, :] = s


def hidden_pair(features, order, pieces, previous, start=(), gates=(), after=()):
    n = len(pieces)
    rows, units = pieces[0].shape
    tokens = features.shape[0]
    kind = jnp.bfloat16 if gates else jnp.float32
    shape = jax.ShapeDtypeStruct((tokens, units), kind)
    anywhere = pl.BlockSpec(memory_space=pl.ANY)
    args = [features, *pieces, previous, *start, *gates, *after]
    wide = pltpu.VMEM((tokens, units), jnp.float32)
    n_more = len(start) + len(gates)
    block = pltpu.VMEM((n, rows, units), jnp.bfloat16)
    return pl.pallas_call(
        functools.partial(hidden_kernel, n, len(start), len(gates), len(after)),
        in_specs=[pl.BlockSpec(memory_space=pltpu.SMEM)] + [anywhere] * len(args),
        out_specs=[pl.BlockSpec(memory_space=pltpu.VMEM)] * 2,
        scratch_shapes=[pltpu.VMEM((n, tokens, rows), jnp.bfloat16), block, block]
        + [wide] * (n_more + 2)
        + [pltpu.VMEM((rows, units), jnp.bfloat16), pltpu.SemaphoreType.DMA((3 * n + n_more,))],
        out_shape=[shape, shape],
        compiler_params=pltpu.CompilerParams(vmem_limit_bytes=VMEM_BYTES),
        cost_estimate=CHEAP,
    )(jnp.stack(order).astype(jnp.int32), *args)


def down_kernel(n, ny, n_after, at, *refs):
    inner = refs[0:2], refs[2:4]
    online, previous = refs[4 : 4 + n], (refs[4 + n : 4 + 2 * n], refs[4 + 2 * n : 4 + 3 * n])
    *gives, keep, w_o, w_t = refs[4 + 3 * n + n_after :]
    tokens, units = inner[0][0].shape
    step = online[0].shape[1]
    for k in range(n):
        here = slice(k * step, (k + 1) * step)
        w_o[:, here] = online[k][...]
        for e in range(2):
            rows = slice(e * units, (e + 1) * units)
            w_t[rows, here] = blend(online[k][rows, :], previous[e][k][...])
    for m, ((own, other), w) in enumerate(zip(inner, (w_o, w_t))):
        s = dot(own[...], w[:units, :]) + dot(other[...], w[units:, :])
        for r, out in enumerate((keep, *gives)):
            rows = slice(r * tokens // ny, (r + 1) * tokens // ny)
            for k in range(n):
                out[at[k], m] = s[rows, k * step : (k + 1) * step].astype(out.dtype)


def down_pair(inner, pieces, blocks, piece_at, old, own_at, other_at, y, step, ny, after):
    n = len(pieces)
    tokens, units = inner[0].shape
    at = [*blocks, *piece_at, *own_at, *other_at, y]
    shape = (n, 2, tokens // ny, step)

    def columns(rows, k, row=lambda w: 0):
        return pl.BlockSpec((rows, step), lambda g, w: (row(w), w[k]))

    return pl.pallas_call(
        functools.partial(down_kernel, n, ny, len(after)),
        grid_spec=pltpu.PrefetchScalarGridSpec(
            num_scalar_prefetch=1,
            grid=(1,),
            in_specs=[pl.BlockSpec((tokens, units), lambda g, w: (0, 0))] * 4
            + [columns(2 * units, n + k) for k in range(n)]
            + [columns(units, 2 * n + k, lambda w: w[4 * n]) for k in range(n)]
            + [columns(units, 3 * n + k) for k in range(n)]
            + [pl.BlockSpec(memory_space=pl.ANY)] * len(after),
            out_specs=[pl.BlockSpec(shape, lambda g, w: (0, 0, 0, 0))] * ny,
            scratch_shapes=[pltpu.VMEM((2 * units, n * step), jnp.bfloat16)] * 2,
        ),
        out_shape=[jax.ShapeDtypeStruct(shape, jnp.bfloat16)] * (ny - 1)
        + [jax.ShapeDtypeStruct(shape, jnp.float32)],
        compiler_params=pltpu.CompilerParams(
            dimension_semantics=("arbitrary",), vmem_limit_bytes=VMEM_BYTES
        ),
        cost_estimate=CHEAP,
    )(
        jnp.stack(at).astype(jnp.int32),
        *inner,
        *pieces,
        *[old[0]] * n,
        *[old[1]] * n,
        *after,
    )


def cut_kernel(at, src, out):
    del at
    out[...] = src[...]


def cut_old(previous, y, h, rows, width):
    n = previous.shape[1] // (2 * width)
    return pl.pallas_call(
        cut_kernel,
        grid_spec=pltpu.PrefetchScalarGridSpec(
            num_scalar_prefetch=1,
            grid=(n,),
            in_specs=[pl.BlockSpec((rows, width), lambda b, at: (at[0], 2 * b + at[1]))],
            out_specs=pl.BlockSpec((rows, width), lambda b, at: (0, b)),
        ),
        out_shape=jax.ShapeDtypeStruct((rows, n * width), previous.dtype),
        cost_estimate=CHEAP,
    )(jnp.stack([y, h]).astype(jnp.int32), previous)


def add_kernel(n_after, keep, *refs):
    *got, out = refs[: len(refs) - 1 - n_after] + refs[-1:]
    total = keep[...]
    for v in got:
        total = total + v[...].astype(jnp.float32)
    out[...] = total.astype(out.dtype)


def add_all(keep, got, after):
    block = pl.BlockSpec((1, *keep.shape[1:]), lambda q: (q, 0, 0, 0))
    return pl.pallas_call(
        functools.partial(add_kernel, len(after)),
        grid=(keep.shape[0],),
        in_specs=[block] * (1 + len(got)) + [pl.BlockSpec(memory_space=pl.ANY)] * len(after),
        out_specs=block,
        out_shape=jax.ShapeDtypeStruct(keep.shape, jnp.bfloat16),
        compiler_params=pltpu.CompilerParams(vmem_limit_bytes=VMEM_BYTES),
        cost_estimate=CHEAP,
    )(keep, *got, *after)


def make_local(n_dp, n_mp):
    ny, nz = n_dp // 2, n_mp // 2
    assert nz == n_dp and n_dp % 2 == 0
    along_x = [(i, i ^ 1) for i in range(n_dp)]
    along_core = [(j, j ^ 1) for j in range(n_mp)]

    def along_y(r):
        return [(y * 2 + x, ((y + r) % ny) * 2 + x) for y in range(ny) for x in range(2)]

    same_core = [[2 * z + c for z in range(nz)] for c in range(2)]

    def local(hidden, gate_on, up_on, down_on, gate_prev, up_prev, down_prev):
        i, j = lax.axis_index("dp"), lax.axis_index("mp")
        y, x = i // 2, i % 2
        c = j % 2
        units = gate_on.shape[1]
        own_units = units // ny
        tokens = hidden.shape[0]

        def before(r):
            return lax.rem(y + (ny - r), ny)

        def swap_units(w, axis):
            out = []
            for r in range(ny):
                start = lax.rem(y + r, ny) * own_units
                piece = lax.dynamic_slice_in_dim(w, start, own_units, axis)
                out.append(piece if r == 0 else lax.ppermute(piece, "dp", along_y(r)))
            return out

        def from_x(pieces):
            return [lax.ppermute(p, "dp", along_x) for p in pieces]

        gate_near = swap_units(gate_on, 1)
        up_near = swap_units(up_on, 1)
        cols = down_on.shape[1]
        half = cols // 2
        down_mine = lax.dynamic_slice_in_dim(down_on, c * half, half, 1)
        down_give = lax.dynamic_slice_in_dim(down_on, (1 - c) * half, half, 1)
        down_pairs = [down_mine, lax.ppermute(down_give, "mp", along_core)]
        down_near = []
        for r in range(ny):
            start = lax.rem(y + r, ny) * own_units
            piece = jnp.concatenate(
                [lax.dynamic_slice_in_dim(w, start, own_units, 0) for w in down_pairs], 0
            )
            down_near.append(piece if r == 0 else lax.ppermute(piece, "dp", along_y(r)))
        gate_far, up_far = from_x(gate_near), from_x(up_near)
        mine = [hidden] + [lax.ppermute(hidden, "dp", along_y(r)) for r in range(1, ny)]
        mine, *_ = lax.optimization_barrier((mine, gate_near[0], up_near[0]))
        features = lax.all_gather(jnp.concatenate(mine, 0), "mp", axis=1, tiled=True)

        near = [before(r) * 2 + x for r in range(ny)]
        far = [before(r) * 2 + (1 - x) for r in range(ny)]
        first = y * own_units
        gate_old, up_old = gate_prev, up_prev
        if own_units % 128:
            gate_old = lax.dynamic_slice_in_dim(gate_prev, first, own_units, 1)
            up_old = lax.dynamic_slice_in_dim(up_prev, first, own_units, 1)
        old_other = lax.ppermute(cut_old(down_prev, y, 1 - c, own_units, half), "mp", along_core)

        gate_part = hidden_pair(features, [*near, first], gate_near, gate_old)
        up_part = hidden_pair(features, [*near, first], up_near, up_old)
        step = 128
        jobs = half // step
        down_send = [
            jnp.concatenate([p[:, s * step : (s + 1) * step] for p in down_near], 1)
            for s in range(jobs)
        ]
        down_far = from_x(down_send)

        gates = hidden_pair(features, [*far, first], gate_far, gate_old, start=gate_part)
        inner_o, inner_t = hidden_pair(
            features,
            [*far, first],
            up_far,
            up_old,
            start=up_part,
            gates=gates,
            after=down_send,
        )

        (inner_o, inner_t), down_far[0] = lax.optimization_barrier(
            ((inner_o, inner_t), down_far[0])
        )
        inner = []
        for v in (inner_o, inner_t):
            inner += [v, lax.ppermute(v, "mp", along_core)]

        def products(s, after):
            *gives, keep = down_pair(
                inner,
                down_near + [down_far[s]] * ny,
                near + far,
                [s + 0 * c] * ny + [k + 0 * c for k in range(ny)],
                (down_prev, old_other),
                [(b * 2 + c) * jobs + s for b in near + far],
                [b * jobs + s for b in near + far],
                y,
                step,
                ny,
                after,
            )
            return keep, gives, [
                lax.ppermute(v, "dp", along_y(ny - 1 - r)) for r, v in enumerate(gives)
            ]

        def over_z(keep, from_y, earlier):
            total = add_all(keep, from_y, earlier)
            summed = lax.psum_scatter(
                total, "mp", scatter_dimension=0, axis_index_groups=same_core, tiled=True
            )
            return total, summed[0]

        results = []
        total, last, waiting = [], [], None
        for s in range(jobs + 1):
            if s < jobs:
                keep, gives, from_y = products(s, last + total)
                last = gives[:1]
            if waiting is not None:
                ahead = last + results[-1:]
                if s + 1 < jobs:
                    ahead.append(down_far[s + 1])
                total, summed = over_z(*waiting, ahead)
                total = [total]
                results.append(summed)
            waiting = keep, from_y
        result = jnp.concatenate(results, -1)
        return result[0], result[1]

    return local


def solution(mesh):
    in_specs = (
        P("dp", "mp"),
        P("dp", "mp"),
        P("dp", "mp"),
        P("mp", "dp"),
        P(None, "mp"),
        P(None, "mp"),
        P("mp", None),
    )
    out_specs = (P("dp", "mp"), P("dp", "mp"))
    local = make_local(mesh.shape["dp"], mesh.shape["mp"])
    return jax.shard_map(local, mesh=mesh, in_specs=in_specs, out_specs=out_specs, check_vma=False)
```

```python
import functools

import jax
import jax.numpy as jnp
from jax import lax
from jax.experimental import pallas as pl
from jax.experimental.pallas import tpu as pltpu
from jax.sharding import PartitionSpec as P

POLYAK = 0.25
TILE = 1024
VMEM_BYTES = 56 * 1024 * 1024
CHEAP = pl.CostEstimate(flops=1, bytes_accessed=1, transcendentals=0)


def blend(online, previous):
    return (
        POLYAK * online.astype(jnp.float32) + (1.0 - POLYAK) * previous.astype(jnp.float32)
    ).astype(jnp.bfloat16)


def dot(a, b):
    return jnp.dot(a, b, preferred_element_type=jnp.float32)


def silu(v):
    return v / (1.0 + jnp.exp(-v))


def hidden_kernel(n, n_start, n_gates, n_after, order, *refs):
    refs = list(refs)

    def take(count):
        out = refs[:count]
        del refs[:count]
        return out

    (features,) = take(1)
    online, (previous,) = take(n), take(1)
    more = take(n_start + n_gates)
    take(n_after)
    outs = take(2)
    f_buf, on_buf, old_buf = take(3)
    more_buf = take(len(more))
    acc = take(2)
    target, sems = take(2)
    rows, units = on_buf.shape[1:]
    tokens = f_buf.shape[1]
    copies = []
    for k in range(n):
        at = pl.ds(pl.multiple_of(order[k] * rows, rows), rows)
        old = previous.at[at]
        if previous.shape[1] != units:
            old = old.at[:, pl.ds(pl.multiple_of(order[n], 128), units)]
        group = [
            pltpu.make_async_copy(online[k], on_buf.at[k], sems.at[3 * k]),
            pltpu.make_async_copy(old, old_buf.at[k], sems.at[3 * k + 1]),
            pltpu.make_async_copy(features.at[:, at], f_buf.at[k], sems.at[3 * k + 2]),
        ]
        for copy in group:
            copy.start()
        copies.append(group)
    last = [
        pltpu.make_async_copy(src, dst, sems.at[3 * n + m])
        for m, (src, dst) in enumerate(zip(more, more_buf))
    ]
    for copy in last:
        copy.start()
    tile = min(TILE, tokens)
    starts = more_buf[:n_start]
    gates = more_buf[n_start:]
    for k in range(n):
        for copy in copies[k]:
            copy.wait()
        target[...] = blend(on_buf[k], old_buf[k])
        if k == n - 1:
            for copy in last:
                copy.wait()

        @pl.loop(0, tokens // tile)
        def _(t):
            here = pl.ds(pl.multiple_of(t * tile, tile), tile)
            f = f_buf[k, here, :]
            for m, w in enumerate((on_buf.at[k], target)):
                s = dot(f, w[...])
                if k > 0:
                    s = s + acc[m][here, :]
                if k == n - 1:
                    if starts:
                        s = s + starts[m][here, :]
                    if gates:
                        s = silu(gates[m][here, :]) * s
                    outs[m][here, :] = s.astype(outs[m].dtype)
                else:
                    acc[m][here, :] = s


def hidden_pair(features, order, pieces, previous, start=(), gates=(), after=()):
    n = len(pieces)
    rows, units = pieces[0].shape
    tokens = features.shape[0]
    kind = jnp.bfloat16 if gates else jnp.float32
    shape = jax.ShapeDtypeStruct((tokens, units), kind)
    anywhere = pl.BlockSpec(memory_space=pl.ANY)
    args = [features, *pieces, previous, *start, *gates, *after]
    wide = pltpu.VMEM((tokens, units), jnp.float32)
    n_more = len(start) + len(gates)
    block = pltpu.VMEM((n, rows, units), jnp.bfloat16)
    return pl.pallas_call(
        functools.partial(hidden_kernel, n, len(start), len(gates), len(after)),
        in_specs=[pl.BlockSpec(memory_space=pltpu.SMEM)] + [anywhere] * len(args),
        out_specs=[pl.BlockSpec(memory_space=pltpu.VMEM)] * 2,
        scratch_shapes=[pltpu.VMEM((n, tokens, rows), jnp.bfloat16), block, block]
        + [wide] * (n_more + 2)
        + [pltpu.VMEM((rows, units), jnp.bfloat16), pltpu.SemaphoreType.DMA((3 * n + n_more,))],
        out_shape=[shape, shape],
        compiler_params=pltpu.CompilerParams(vmem_limit_bytes=VMEM_BYTES),
        cost_estimate=CHEAP,
    )(jnp.stack(order).astype(jnp.int32), *args)


def down_kernel(n, ny, n_after, at, *refs):
    inner = refs[0:2], refs[2:4]
    online, previous = refs[4 : 4 + n], (refs[4 + n : 4 + 2 * n], refs[4 + 2 * n : 4 + 3 * n])
    *gives, keep, w_o, w_t = refs[4 + 3 * n + n_after :]
    tokens, units = inner[0][0].shape
    step = online[0].shape[1]
    for k in range(n):
        here = slice(k * step, (k + 1) * step)
        w_o[:, here] = online[k][...]
        for e in range(2):
            rows = slice(e * units, (e + 1) * units)
            w_t[rows, here] = blend(online[k][rows, :], previous[e][k][...])
    for m, ((own, other), w) in enumerate(zip(inner, (w_o, w_t))):
        s = dot(own[...], w[:units, :]) + dot(other[...], w[units:, :])
        for r, out in enumerate((keep, *gives)):
            rows = slice(r * tokens // ny, (r + 1) * tokens // ny)
            for k in range(n):
                out[at[k], m] = s[rows, k * step : (k + 1) * step].astype(out.dtype)


def down_pair(inner, pieces, blocks, piece_at, old, own_at, other_at, y, step, ny, after):
    n = len(pieces)
    tokens, units = inner[0].shape
    at = [*blocks, *piece_at, *own_at, *other_at, y]
    shape = (n, 2, tokens // ny, step)

    def columns(rows, k, row=lambda w: 0):
        return pl.BlockSpec((rows, step), lambda g, w: (row(w), w[k]))

    return pl.pallas_call(
        functools.partial(down_kernel, n, ny, len(after)),
        grid_spec=pltpu.PrefetchScalarGridSpec(
            num_scalar_prefetch=1,
            grid=(1,),
            in_specs=[pl.BlockSpec((tokens, units), lambda g, w: (0, 0))] * 4
            + [columns(2 * units, n + k) for k in range(n)]
            + [columns(units, 2 * n + k, lambda w: w[4 * n]) for k in range(n)]
            + [columns(units, 3 * n + k) for k in range(n)]
            + [pl.BlockSpec(memory_space=pl.ANY)] * len(after),
            out_specs=[pl.BlockSpec(shape, lambda g, w: (0, 0, 0, 0))] * ny,
            scratch_shapes=[pltpu.VMEM((2 * units, n * step), jnp.bfloat16)] * 2,
        ),
        out_shape=[jax.ShapeDtypeStruct(shape, jnp.bfloat16)] * (ny - 1)
        + [jax.ShapeDtypeStruct(shape, jnp.float32)],
        compiler_params=pltpu.CompilerParams(
            dimension_semantics=("arbitrary",), vmem_limit_bytes=VMEM_BYTES
        ),
        cost_estimate=CHEAP,
    )(
        jnp.stack(at).astype(jnp.int32),
        *inner,
        *pieces,
        *[old[0]] * n,
        *[old[1]] * n,
        *after,
    )


def cut_kernel(at, src, out):
    del at
    out[...] = src[...]


def cut_old(previous, y, h, rows, width):
    n = previous.shape[1] // (2 * width)
    return pl.pallas_call(
        cut_kernel,
        grid_spec=pltpu.PrefetchScalarGridSpec(
            num_scalar_prefetch=1,
            grid=(n,),
            in_specs=[pl.BlockSpec((rows, width), lambda b, at: (at[0], 2 * b + at[1]))],
            out_specs=pl.BlockSpec((rows, width), lambda b, at: (0, b)),
        ),
        out_shape=jax.ShapeDtypeStruct((rows, n * width), previous.dtype),
        cost_estimate=CHEAP,
    )(jnp.stack([y, h]).astype(jnp.int32), previous)


def make_local(n_dp, n_mp):
    ny, nz = n_dp // 2, n_mp // 2
    assert nz == n_dp and n_dp % 2 == 0
    along_x = [(i, i ^ 1) for i in range(n_dp)]
    along_core = [(j, j ^ 1) for j in range(n_mp)]

    def along_y(r):
        return [(y * 2 + x, ((y + r) % ny) * 2 + x) for y in range(ny) for x in range(2)]

    same_core = [[2 * z + c for z in range(nz)] for c in range(2)]

    def local(hidden, gate_on, up_on, down_on, gate_prev, up_prev, down_prev):
        i, j = lax.axis_index("dp"), lax.axis_index("mp")
        y, x = i // 2, i % 2
        c = j % 2
        units = gate_on.shape[1]
        own_units = units // ny
        tokens = hidden.shape[0]

        def before(r):
            return lax.rem(y + (ny - r), ny)

        def swap_units(w, axis):
            out = []
            for r in range(ny):
                start = lax.rem(y + r, ny) * own_units
                piece = lax.dynamic_slice_in_dim(w, start, own_units, axis)
                out.append(piece if r == 0 else lax.ppermute(piece, "dp", along_y(r)))
            return out

        def from_x(pieces):
            return [lax.ppermute(p, "dp", along_x) for p in pieces]

        gate_near = swap_units(gate_on, 1)
        up_near = swap_units(up_on, 1)
        gate_far, up_far = from_x(gate_near), from_x(up_near)
        cols = down_on.shape[1]
        half = cols // 2
        (down_on, down_prev), _ = lax.optimization_barrier(
            ((down_on, down_prev), (gate_near[1:], up_near[1:], gate_far[0], up_far[0]))
        )
        down_mine = lax.dynamic_slice_in_dim(down_on, c * half, half, 1)
        down_give = lax.dynamic_slice_in_dim(down_on, (1 - c) * half, half, 1)
        down_pairs = [down_mine, lax.ppermute(down_give, "mp", along_core)]
        down_near = []
        for r in range(ny):
            start = lax.rem(y + r, ny) * own_units
            piece = jnp.concatenate(
                [lax.dynamic_slice_in_dim(w, start, own_units, 0) for w in down_pairs], 0
            )
            down_near.append(piece if r == 0 else lax.ppermute(piece, "dp", along_y(r)))
        mine = [hidden] + [lax.ppermute(hidden, "dp", along_y(r)) for r in range(1, ny)]
        mine, *_ = lax.optimization_barrier((mine, gate_near[0], up_near[0]))
        features = lax.all_gather(jnp.concatenate(mine, 0), "mp", axis=1, tiled=True)

        near = [before(r) * 2 + x for r in range(ny)]
        far = [before(r) * 2 + (1 - x) for r in range(ny)]
        first = y * own_units
        gate_old, up_old = gate_prev, up_prev
        if own_units % 128:
            gate_old = lax.dynamic_slice_in_dim(gate_prev, first, own_units, 1)
            up_old = lax.dynamic_slice_in_dim(up_prev, first, own_units, 1)
        old_other = lax.ppermute(cut_old(down_prev, y, 1 - c, own_units, half), "mp", along_core)

        gate_part = hidden_pair(features, [*near, first], gate_near, gate_old)
        up_part = hidden_pair(features, [*near, first], up_near, up_old)
        down_near, _ = lax.optimization_barrier((down_near, (gate_part, up_part)))

        step = 128
        jobs = half // step
        down_send = [
            jnp.concatenate([p[:, s * step : (s + 1) * step] for p in down_near], 1)
            for s in range(jobs)
        ]
        down_far = from_x(down_send)

        gates = hidden_pair(features, [*far, first], gate_far, gate_old, start=gate_part)
        inner_o, inner_t = hidden_pair(
            features,
            [*far, first],
            up_far,
            up_old,
            start=up_part,
            gates=gates,
            after=down_send + down_near,
        )

        (inner_o, inner_t), down_far[0] = lax.optimization_barrier(
            ((inner_o, inner_t), down_far[0])
        )
        inner = []
        for v in (inner_o, inner_t):
            inner += [v, lax.ppermute(v, "mp", along_core)]

        def products(s, after):
            *gives, keep = down_pair(
                inner,
                down_near + [down_far[s]] * ny,
                near + far,
                [s + 0 * c] * ny + [k + 0 * c for k in range(ny)],
                (down_prev, old_other),
                [(b * 2 + c) * jobs + s for b in near + far],
                [b * jobs + s for b in near + far],
                y,
                step,
                ny,
                after,
            )
            if s + 1 < jobs:
                gives, down_far[s + 1] = lax.optimization_barrier((gives, down_far[s + 1]))
            return keep, gives, [
                lax.ppermute(v, "dp", along_y(ny - 1 - r)) for r, v in enumerate(gives)
            ]

        def over_z(keep, from_y, after, earlier):
            (keep, from_y), _ = lax.optimization_barrier(((keep, from_y), after))
            total = keep
            for v in from_y:
                total = total + v.astype(jnp.float32)
            total, _ = lax.optimization_barrier((total.astype(jnp.bfloat16), earlier))
            summed = lax.psum_scatter(
                total, "mp", scatter_dimension=0, axis_index_groups=same_core, tiled=True
            )
            return total, summed[0]

        results = []
        total, last, waiting = [], [], None
        for s in range(jobs + 1):
            if s < jobs:
                keep, gives, from_y = products(s, last + total)
                last = gives[:1]
            if waiting is not None:
                total, summed = over_z(*waiting, last, results[-1:])
                total = [total]
                results.append(summed)
            waiting = keep, from_y
        result = jnp.concatenate(results, -1)
        return result[0], result[1]

    return local


def solution(mesh):
    in_specs = (
        P("dp", "mp"),
        P("dp", "mp"),
        P("dp", "mp"),
        P("mp", "dp"),
        P(None, "mp"),
        P(None, "mp"),
        P("mp", None),
    )
    out_specs = (P("dp", "mp"), P("dp", "mp"))
    local = make_local(mesh.shape["dp"], mesh.shape["mp"])
    return jax.shard_map(local, mesh=mesh, in_specs=in_specs, out_specs=out_specs, check_vma=False)
```

```python
import functools

import jax
import jax.numpy as jnp
from jax import lax
from jax.experimental import pallas as pl
from jax.experimental.pallas import tpu as pltpu
from jax.sharding import PartitionSpec as P

POLYAK = 0.25
TILE = 1024
VMEM_BYTES = 56 * 1024 * 1024
CHEAP = pl.CostEstimate(flops=1, bytes_accessed=1, transcendentals=0)


def blend(online, previous):
    return (
        POLYAK * online.astype(jnp.float32) + (1.0 - POLYAK) * previous.astype(jnp.float32)
    ).astype(jnp.bfloat16)


def dot(a, b):
    return jnp.dot(a, b, preferred_element_type=jnp.float32)


def silu(v):
    return v / (1.0 + jnp.exp(-v))


def hidden_kernel(n, n_start, n_gates, n_after, act, order, *refs):
    refs = list(refs)

    def take(count):
        out = refs[:count]
        del refs[:count]
        return out

    (features,) = take(1)
    online, (previous,) = take(n), take(1)
    more = take(n_start + n_gates)
    take(n_after)
    outs = take(2)
    f_buf, on_buf, old_buf = take(3)
    more_buf = take(len(more))
    acc = take(2)
    target, sems = take(2)
    rows, units = on_buf.shape[1:]
    tokens = f_buf.shape[1]
    copies = []
    for k in range(n):
        at = pl.ds(pl.multiple_of(order[k] * rows, rows), rows)
        old = previous.at[at]
        if previous.shape[1] != units:
            old = old.at[:, pl.ds(pl.multiple_of(order[n], 128), units)]
        group = [
            pltpu.make_async_copy(online[k], on_buf.at[k], sems.at[3 * k]),
            pltpu.make_async_copy(old, old_buf.at[k], sems.at[3 * k + 1]),
            pltpu.make_async_copy(features.at[:, at], f_buf.at[k], sems.at[3 * k + 2]),
        ]
        for copy in group:
            copy.start()
        copies.append(group)
    last = [
        pltpu.make_async_copy(src, dst, sems.at[3 * n + m])
        for m, (src, dst) in enumerate(zip(more, more_buf))
    ]
    for copy in last:
        copy.start()
    tile = min(TILE, tokens)
    starts = more_buf[:n_start]
    gates = more_buf[n_start:]
    for k in range(n):
        for copy in copies[k]:
            copy.wait()
        target[...] = blend(on_buf[k], old_buf[k])
        if k == n - 1:
            for copy in last:
                copy.wait()

        @pl.loop(0, tokens // tile)
        def _(t):
            here = pl.ds(pl.multiple_of(t * tile, tile), tile)
            f = f_buf[k, here, :]
            for m, w in enumerate((on_buf.at[k], target)):
                s = dot(f, w[...])
                if k > 0:
                    s = s + acc[m][here, :]
                if k == n - 1:
                    if starts:
                        s = s + starts[m][here, :]
                    if act:
                        s = silu(s)
                    if gates:
                        s = gates[m][here, :] * s
                    outs[m][here, :] = s.astype(outs[m].dtype)
                else:
                    acc[m][here, :] = s


def hidden_pair(features, order, pieces, previous, start=(), gates=(), after=(), act=False):
    n = len(pieces)
    rows, units = pieces[0].shape
    tokens = features.shape[0]
    kind = jnp.bfloat16 if gates else jnp.float32
    shape = jax.ShapeDtypeStruct((tokens, units), kind)
    anywhere = pl.BlockSpec(memory_space=pl.ANY)
    args = [features, *pieces, previous, *start, *gates, *after]
    wide = pltpu.VMEM((tokens, units), jnp.float32)
    n_more = len(start) + len(gates)
    block = pltpu.VMEM((n, rows, units), jnp.bfloat16)
    return pl.pallas_call(
        functools.partial(hidden_kernel, n, len(start), len(gates), len(after), act),
        in_specs=[pl.BlockSpec(memory_space=pltpu.SMEM)] + [anywhere] * len(args),
        out_specs=[pl.BlockSpec(memory_space=pltpu.VMEM)] * 2,
        scratch_shapes=[pltpu.VMEM((n, tokens, rows), jnp.bfloat16), block, block]
        + [wide] * (n_more + 2)
        + [pltpu.VMEM((rows, units), jnp.bfloat16), pltpu.SemaphoreType.DMA((3 * n + n_more,))],
        out_shape=[shape, shape],
        compiler_params=pltpu.CompilerParams(vmem_limit_bytes=VMEM_BYTES),
        cost_estimate=CHEAP,
    )(jnp.stack(order).astype(jnp.int32), *args)


def down_kernel(n, ny, n_after, at, *refs):
    inner = refs[0:2], refs[2:4]
    online, previous = refs[4 : 4 + n], (refs[4 + n : 4 + 2 * n], refs[4 + 2 * n : 4 + 3 * n])
    *gives, keep, w_o, w_t = refs[4 + 3 * n + n_after :]
    tokens, units = inner[0][0].shape
    step = online[0].shape[1]
    for k in range(n):
        here = slice(k * step, (k + 1) * step)
        w_o[:, here] = online[k][...]
        for e in range(2):
            rows = slice(e * units, (e + 1) * units)
            w_t[rows, here] = blend(online[k][rows, :], previous[e][k][...])
    for m, ((own, other), w) in enumerate(zip(inner, (w_o, w_t))):
        s = dot(own[...], w[:units, :]) + dot(other[...], w[units:, :])
        for r, out in enumerate((keep, *gives)):
            rows = slice(r * tokens // ny, (r + 1) * tokens // ny)
            for k in range(n):
                out[at[k], m] = s[rows, k * step : (k + 1) * step].astype(out.dtype)


def down_pair(inner, pieces, blocks, piece_at, old, own_at, other_at, y, step, ny, after):
    n = len(pieces)
    tokens, units = inner[0].shape
    at = [*blocks, *piece_at, *own_at, *other_at, y]
    shape = (n, 2, tokens // ny, step)

    def columns(rows, k, row=lambda w: 0):
        return pl.BlockSpec((rows, step), lambda g, w: (row(w), w[k]))

    return pl.pallas_call(
        functools.partial(down_kernel, n, ny, len(after)),
        grid_spec=pltpu.PrefetchScalarGridSpec(
            num_scalar_prefetch=1,
            grid=(1,),
            in_specs=[pl.BlockSpec((tokens, units), lambda g, w: (0, 0))] * 4
            + [columns(2 * units, n + k) for k in range(n)]
            + [columns(units, 2 * n + k, lambda w: w[4 * n]) for k in range(n)]
            + [columns(units, 3 * n + k) for k in range(n)]
            + [pl.BlockSpec(memory_space=pl.ANY)] * len(after),
            out_specs=[pl.BlockSpec(shape, lambda g, w: (0, 0, 0, 0))] * ny,
            scratch_shapes=[pltpu.VMEM((2 * units, n * step), jnp.bfloat16)] * 2,
        ),
        out_shape=[jax.ShapeDtypeStruct(shape, jnp.bfloat16)] * (ny - 1)
        + [jax.ShapeDtypeStruct(shape, jnp.float32)],
        compiler_params=pltpu.CompilerParams(
            dimension_semantics=("arbitrary",), vmem_limit_bytes=VMEM_BYTES
        ),
        cost_estimate=CHEAP,
    )(
        jnp.stack(at).astype(jnp.int32),
        *inner,
        *pieces,
        *[old[0]] * n,
        *[old[1]] * n,
        *after,
    )


def cut_kernel(at, src, out):
    del at
    out[...] = src[...]


def cut_old(previous, y, h, rows, width):
    n = previous.shape[1] // (2 * width)
    return pl.pallas_call(
        cut_kernel,
        grid_spec=pltpu.PrefetchScalarGridSpec(
            num_scalar_prefetch=1,
            grid=(n,),
            in_specs=[pl.BlockSpec((rows, width), lambda b, at: (at[0], 2 * b + at[1]))],
            out_specs=pl.BlockSpec((rows, width), lambda b, at: (0, b)),
        ),
        out_shape=jax.ShapeDtypeStruct((rows, n * width), previous.dtype),
        cost_estimate=CHEAP,
    )(jnp.stack([y, h]).astype(jnp.int32), previous)


def make_local(n_dp, n_mp):
    ny, nz = n_dp // 2, n_mp // 2
    assert nz == n_dp and n_dp % 2 == 0
    along_x = [(i, i ^ 1) for i in range(n_dp)]
    along_core = [(j, j ^ 1) for j in range(n_mp)]

    def along_y(r):
        return [(y * 2 + x, ((y + r) % ny) * 2 + x) for y in range(ny) for x in range(2)]

    same_core = [[2 * z + c for z in range(nz)] for c in range(2)]

    def local(hidden, gate_on, up_on, down_on, gate_prev, up_prev, down_prev):
        i, j = lax.axis_index("dp"), lax.axis_index("mp")
        y, x = i // 2, i % 2
        c = j % 2
        units = gate_on.shape[1]
        own_units = units // ny
        tokens = hidden.shape[0]

        def before(r):
            return lax.rem(y + (ny - r), ny)

        def swap_units(w, axis):
            out = []
            for r in range(ny):
                start = lax.rem(y + r, ny) * own_units
                piece = lax.dynamic_slice_in_dim(w, start, own_units, axis)
                out.append(piece if r == 0 else lax.ppermute(piece, "dp", along_y(r)))
            return out

        def from_x(pieces):
            return [lax.ppermute(p, "dp", along_x) for p in pieces]

        gate_near = swap_units(gate_on, 1)
        up_near = swap_units(up_on, 1)
        gate_far, up_far = from_x(gate_near), from_x(up_near)
        cols = down_on.shape[1]
        half = cols // 2
        down_mine = lax.dynamic_slice_in_dim(down_on, c * half, half, 1)
        down_give = lax.dynamic_slice_in_dim(down_on, (1 - c) * half, half, 1)
        down_pairs = [down_mine, lax.ppermute(down_give, "mp", along_core)]
        (down_pairs, down_prev), _ = lax.optimization_barrier(
            ((down_pairs, down_prev), (gate_near[1:], up_near[1:], gate_far[0], up_far[0]))
        )
        down_near = []
        for r in range(ny):
            start = lax.rem(y + r, ny) * own_units
            piece = jnp.concatenate(
                [lax.dynamic_slice_in_dim(w, start, own_units, 0) for w in down_pairs], 0
            )
            down_near.append(piece if r == 0 else lax.ppermute(piece, "dp", along_y(r)))
        mine = [hidden] + [lax.ppermute(hidden, "dp", along_y(r)) for r in range(1, ny)]
        mine, *_ = lax.optimization_barrier((mine, gate_near[0], up_near[0]))
        features = lax.all_gather(jnp.concatenate(mine, 0), "mp", axis=1, tiled=True)

        near = [before(r) * 2 + x for r in range(ny)]
        far = [before(r) * 2 + (1 - x) for r in range(ny)]
        first = y * own_units
        gate_old, up_old = gate_prev, up_prev
        if own_units % 128:
            gate_old = lax.dynamic_slice_in_dim(gate_prev, first, own_units, 1)
            up_old = lax.dynamic_slice_in_dim(up_prev, first, own_units, 1)
        old_other = lax.ppermute(cut_old(down_prev, y, 1 - c, own_units, half), "mp", along_core)

        gate_part = hidden_pair(features, [*near, first], gate_near, gate_old)
        up_part = hidden_pair(features, [*near, first], up_near, up_old)
        down_near, _ = lax.optimization_barrier((down_near, (gate_part, up_part)))

        step = 128
        jobs = half // step
        down_send = [
            jnp.concatenate([p[:, s * step : (s + 1) * step] for p in down_near], 1)
            for s in range(jobs)
        ]
        down_far = from_x(down_send)

        gates = hidden_pair(features, [*far, first], gate_far, gate_old, start=gate_part, act=True)
        inner_o, inner_t = hidden_pair(
            features,
            [*far, first],
            up_far,
            up_old,
            start=up_part,
            gates=gates,
            after=down_send + down_near,
        )

        (inner_o, inner_t), down_far[0] = lax.optimization_barrier(
            ((inner_o, inner_t), down_far[0])
        )
        inner = []
        for v in (inner_o, inner_t):
            inner += [v, lax.ppermute(v, "mp", along_core)]

        def products(s, after):
            *gives, keep = down_pair(
                inner,
                down_near + [down_far[s]] * ny,
                near + far,
                [s + 0 * c] * ny + [k + 0 * c for k in range(ny)],
                (down_prev, old_other),
                [(b * 2 + c) * jobs + s for b in near + far],
                [b * jobs + s for b in near + far],
                y,
                step,
                ny,
                after,
            )
            if s + 1 < jobs:
                gives, down_far[s + 1] = lax.optimization_barrier((gives, down_far[s + 1]))
            return keep, gives, [
                lax.ppermute(v, "dp", along_y(ny - 1 - r)) for r, v in enumerate(gives)
            ]

        def over_z(keep, from_y, after, earlier):
            (keep, from_y), _ = lax.optimization_barrier(((keep, from_y), after))
            total = keep
            for v in from_y:
                total = total + v.astype(jnp.float32)
            total, _ = lax.optimization_barrier((total.astype(jnp.bfloat16), earlier))
            summed = lax.psum_scatter(
                total, "mp", scatter_dimension=0, axis_index_groups=same_core, tiled=True
            )
            return total, summed[0]

        results = []
        total, last, waiting = [], [], None
        for s in range(jobs + 1):
            if s < jobs:
                keep, gives, from_y = products(s, last + total)
                last = gives[:1]
            if waiting is not None:
                total, summed = over_z(*waiting, last, results[-1:])
                total = [total]
                results.append(summed)
            waiting = keep, from_y
        result = jnp.concatenate(results, -1)
        return result[0], result[1]

    return local


def solution(mesh):
    in_specs = (
        P("dp", "mp"),
        P("dp", "mp"),
        P("dp", "mp"),
        P("mp", "dp"),
        P(None, "mp"),
        P(None, "mp"),
        P("mp", None),
    )
    out_specs = (P("dp", "mp"), P("dp", "mp"))
    local = make_local(mesh.shape["dp"], mesh.shape["mp"])
    return jax.shard_map(local, mesh=mesh, in_specs=in_specs, out_specs=out_specs, check_vma=False)
```

```python
import functools

import jax
import jax.numpy as jnp
from jax import lax
from jax.experimental import pallas as pl
from jax.experimental.pallas import tpu as pltpu
from jax.sharding import PartitionSpec as P

POLYAK = 0.25
TILE = 1024
VMEM_BYTES = 56 * 1024 * 1024
CHEAP = pl.CostEstimate(flops=1, bytes_accessed=1, transcendentals=0)


def blend(online, previous):
    return (
        POLYAK * online.astype(jnp.float32) + (1.0 - POLYAK) * previous.astype(jnp.float32)
    ).astype(jnp.bfloat16)


def dot(a, b):
    return jnp.dot(a, b, preferred_element_type=jnp.float32)


def silu(v):
    return v / (1.0 + jnp.exp(-v))


def hidden_kernel(n, n_start, n_gates, n_after, act, order, *refs):
    refs = list(refs)

    def take(count):
        out = refs[:count]
        del refs[:count]
        return out

    (features,) = take(1)
    online, (previous,) = take(n), take(1)
    more = take(n_start + n_gates)
    take(n_after)
    outs = take(2)
    f_buf, on_buf, old_buf = take(3)
    more_buf = take(len(more))
    acc = take(2)
    target, sems = take(2)
    rows, units = on_buf.shape[1:]
    tokens = f_buf.shape[1]
    copies = []
    for k in range(n):
        at = pl.ds(pl.multiple_of(order[k] * rows, rows), rows)
        old = previous.at[at]
        if previous.shape[1] != units:
            old = old.at[:, pl.ds(pl.multiple_of(order[n], 128), units)]
        group = [
            pltpu.make_async_copy(online[k], on_buf.at[k], sems.at[3 * k]),
            pltpu.make_async_copy(old, old_buf.at[k], sems.at[3 * k + 1]),
            pltpu.make_async_copy(features.at[:, at], f_buf.at[k], sems.at[3 * k + 2]),
        ]
        for copy in group:
            copy.start()
        copies.append(group)
    last = [
        pltpu.make_async_copy(src, dst, sems.at[3 * n + m])
        for m, (src, dst) in enumerate(zip(more, more_buf))
    ]
    for copy in last:
        copy.start()
    tile = min(TILE, tokens)
    starts = more_buf[:n_start]
    gates = more_buf[n_start:]
    for k in range(n):
        for copy in copies[k]:
            copy.wait()
        target[...] = blend(on_buf[k], old_buf[k])
        if k == n - 1:
            for copy in last:
                copy.wait()

        @pl.loop(0, tokens // tile)
        def _(t):
            here = pl.ds(pl.multiple_of(t * tile, tile), tile)
            f = f_buf[k, here, :]
            for m, w in enumerate((on_buf.at[k], target)):
                s = dot(f, w[...])
                if k > 0:
                    s = s + acc[m][here, :]
                if k == n - 1:
                    if starts:
                        s = s + starts[m][here, :]
                    if act:
                        s = silu(s)
                    if gates:
                        s = gates[m][here, :] * s
                    outs[m][here, :] = s.astype(outs[m].dtype)
                else:
                    acc[m][here, :] = s


def hidden_pair(features, order, pieces, previous, start=(), gates=(), after=(), act=False):
    n = len(pieces)
    rows, units = pieces[0].shape
    tokens = features.shape[0]
    kind = jnp.bfloat16 if gates else jnp.float32
    shape = jax.ShapeDtypeStruct((tokens, units), kind)
    anywhere = pl.BlockSpec(memory_space=pl.ANY)
    args = [features, *pieces, previous, *start, *gates, *after]
    wide = pltpu.VMEM((tokens, units), jnp.float32)
    n_more = len(start) + len(gates)
    block = pltpu.VMEM((n, rows, units), jnp.bfloat16)
    return pl.pallas_call(
        functools.partial(hidden_kernel, n, len(start), len(gates), len(after), act),
        in_specs=[pl.BlockSpec(memory_space=pltpu.SMEM)] + [anywhere] * len(args),
        out_specs=[pl.BlockSpec(memory_space=pltpu.VMEM)] * 2,
        scratch_shapes=[pltpu.VMEM((n, tokens, rows), jnp.bfloat16), block, block]
        + [wide] * (n_more + 2)
        + [pltpu.VMEM((rows, units), jnp.bfloat16), pltpu.SemaphoreType.DMA((3 * n + n_more,))],
        out_shape=[shape, shape],
        compiler_params=pltpu.CompilerParams(vmem_limit_bytes=VMEM_BYTES),
        cost_estimate=CHEAP,
    )(jnp.stack(order).astype(jnp.int32), *args)


def down_kernel(n, ny, n_after, at, *refs):
    inner = refs[0:2], refs[2:4]
    online, previous = refs[4 : 4 + n], (refs[4 + n : 4 + 2 * n], refs[4 + 2 * n : 4 + 3 * n])
    *gives, keep, w_o, w_t = refs[4 + 3 * n + n_after :]
    tokens, units = inner[0][0].shape
    step = online[0].shape[1]
    for k in range(n):
        here = slice(k * step, (k + 1) * step)
        w_o[:, here] = online[k][...]
        for e in range(2):
            rows = slice(e * units, (e + 1) * units)
            w_t[rows, here] = blend(online[k][rows, :], previous[e][k][...])
    for m, ((own, other), w) in enumerate(zip(inner, (w_o, w_t))):
        s = dot(own[...], w[:units, :]) + dot(other[...], w[units:, :])
        for r, out in enumerate((keep, *gives)):
            rows = slice(r * tokens // ny, (r + 1) * tokens // ny)
            for k in range(n):
                out[at[k], m] = s[rows, k * step : (k + 1) * step].astype(out.dtype)


def down_pair(inner, pieces, blocks, piece_at, old, own_at, other_at, y, step, ny, after):
    n = len(pieces)
    tokens, units = inner[0].shape
    at = [*blocks, *piece_at, *own_at, *other_at, y]
    shape = (n, 2, tokens // ny, step)

    def columns(rows, k, row=lambda w: 0):
        return pl.BlockSpec((rows, step), lambda g, w: (row(w), w[k]))

    return pl.pallas_call(
        functools.partial(down_kernel, n, ny, len(after)),
        grid_spec=pltpu.PrefetchScalarGridSpec(
            num_scalar_prefetch=1,
            grid=(1,),
            in_specs=[pl.BlockSpec((tokens, units), lambda g, w: (0, 0))] * 4
            + [columns(2 * units, n + k) for k in range(n)]
            + [columns(units, 2 * n + k, lambda w: w[4 * n]) for k in range(n)]
            + [columns(units, 3 * n + k) for k in range(n)]
            + [pl.BlockSpec(memory_space=pl.ANY)] * len(after),
            out_specs=[pl.BlockSpec(shape, lambda g, w: (0, 0, 0, 0))] * ny,
            scratch_shapes=[pltpu.VMEM((2 * units, n * step), jnp.bfloat16)] * 2,
        ),
        out_shape=[jax.ShapeDtypeStruct(shape, jnp.bfloat16)] * (ny - 1)
        + [jax.ShapeDtypeStruct(shape, jnp.float32)],
        compiler_params=pltpu.CompilerParams(
            dimension_semantics=("arbitrary",), vmem_limit_bytes=VMEM_BYTES
        ),
        cost_estimate=CHEAP,
    )(
        jnp.stack(at).astype(jnp.int32),
        *inner,
        *pieces,
        *[old[0]] * n,
        *[old[1]] * n,
        *after,
    )


def cut_kernel(at, src, out):
    del at
    out[...] = src[...]


def cut_old(previous, y, h, rows, width):
    n = previous.shape[1] // (2 * width)
    return pl.pallas_call(
        cut_kernel,
        grid_spec=pltpu.PrefetchScalarGridSpec(
            num_scalar_prefetch=1,
            grid=(n,),
            in_specs=[pl.BlockSpec((rows, width), lambda b, at: (at[0], 2 * b + at[1]))],
            out_specs=pl.BlockSpec((rows, width), lambda b, at: (0, b)),
        ),
        out_shape=jax.ShapeDtypeStruct((rows, n * width), previous.dtype),
        cost_estimate=CHEAP,
    )(jnp.stack([y, h]).astype(jnp.int32), previous)


def make_local(n_dp, n_mp):
    ny, nz = n_dp // 2, n_mp // 2
    assert nz == n_dp and n_dp % 2 == 0
    along_x = [(i, i ^ 1) for i in range(n_dp)]
    along_core = [(j, j ^ 1) for j in range(n_mp)]

    def along_y(r):
        return [(y * 2 + x, ((y + r) % ny) * 2 + x) for y in range(ny) for x in range(2)]

    same_core = [[2 * z + c for z in range(nz)] for c in range(2)]

    def local(hidden, gate_on, up_on, down_on, gate_prev, up_prev, down_prev):
        i, j = lax.axis_index("dp"), lax.axis_index("mp")
        y, x = i // 2, i % 2
        c = j % 2
        units = gate_on.shape[1]
        own_units = units // ny
        tokens = hidden.shape[0]

        def before(r):
            return lax.rem(y + (ny - r), ny)

        def swap_units(w, axis):
            out = []
            for r in range(ny):
                start = lax.rem(y + r, ny) * own_units
                piece = lax.dynamic_slice_in_dim(w, start, own_units, axis)
                out.append(piece if r == 0 else lax.ppermute(piece, "dp", along_y(r)))
            return out

        def from_x(pieces):
            return [lax.ppermute(p, "dp", along_x) for p in pieces]

        gate_near = swap_units(gate_on, 1)
        up_near = swap_units(up_on, 1)
        gate_far, up_far = from_x(gate_near), from_x(up_near)
        cols = down_on.shape[1]
        half = cols // 2
        down_mine = lax.dynamic_slice_in_dim(down_on, c * half, half, 1)
        down_give = lax.dynamic_slice_in_dim(down_on, (1 - c) * half, half, 1)
        down_pairs = [down_mine, lax.ppermute(down_give, "mp", along_core)]
        down_pairs, _ = lax.optimization_barrier(
            (down_pairs, (gate_near[1:], up_near[1:], gate_far[0], up_far[0]))
        )
        down_prev, _ = lax.optimization_barrier((down_prev, (gate_near[1:], gate_far[0])))
        down_near = []
        for r in range(ny):
            start = lax.rem(y + r, ny) * own_units
            piece = jnp.concatenate(
                [lax.dynamic_slice_in_dim(w, start, own_units, 0) for w in down_pairs], 0
            )
            down_near.append(piece if r == 0 else lax.ppermute(piece, "dp", along_y(r)))
        mine = [hidden] + [lax.ppermute(hidden, "dp", along_y(r)) for r in range(1, ny)]
        mine, *_ = lax.optimization_barrier((mine, gate_near[0], up_near[0]))
        features = lax.all_gather(jnp.concatenate(mine, 0), "mp", axis=1, tiled=True)

        near = [before(r) * 2 + x for r in range(ny)]
        far = [before(r) * 2 + (1 - x) for r in range(ny)]
        first = y * own_units
        gate_old, up_old = gate_prev, up_prev
        if own_units % 128:
            gate_old = lax.dynamic_slice_in_dim(gate_prev, first, own_units, 1)
            up_old = lax.dynamic_slice_in_dim(up_prev, first, own_units, 1)
        old_other = lax.ppermute(cut_old(down_prev, y, 1 - c, own_units, half), "mp", along_core)

        gate_part = hidden_pair(features, [*near, first], gate_near, gate_old)
        up_part = hidden_pair(features, [*near, first], up_near, up_old)
        down_near, _ = lax.optimization_barrier((down_near, (gate_part, up_part)))

        step = 128
        jobs = half // step
        down_send = [
            jnp.concatenate([p[:, s * step : (s + 1) * step] for p in down_near], 1)
            for s in range(jobs)
        ]
        down_far = from_x(down_send)

        gates = hidden_pair(features, [*far, first], gate_far, gate_old, start=gate_part, act=True)
        inner_o, inner_t = hidden_pair(
            features,
            [*far, first],
            up_far,
            up_old,
            start=up_part,
            gates=gates,
            after=down_send + down_near,
        )

        (inner_o, inner_t), down_far[0] = lax.optimization_barrier(
            ((inner_o, inner_t), down_far[0])
        )
        inner = []
        for v in (inner_o, inner_t):
            inner += [v, lax.ppermute(v, "mp", along_core)]

        def products(s, after):
            *gives, keep = down_pair(
                inner,
                down_near + [down_far[s]] * ny,
                near + far,
                [s + 0 * c] * ny + [k + 0 * c for k in range(ny)],
                (down_prev, old_other),
                [(b * 2 + c) * jobs + s for b in near + far],
                [b * jobs + s for b in near + far],
                y,
                step,
                ny,
                after,
            )
            if s + 1 < jobs:
                gives, down_far[s + 1] = lax.optimization_barrier((gives, down_far[s + 1]))
            return keep, gives, [
                lax.ppermute(v, "dp", along_y(ny - 1 - r)) for r, v in enumerate(gives)
            ]

        def over_z(keep, from_y, after, earlier):
            (keep, from_y), _ = lax.optimization_barrier(((keep, from_y), after))
            total = keep
            for v in from_y:
                total = total + v.astype(jnp.float32)
            total, _ = lax.optimization_barrier((total.astype(jnp.bfloat16), earlier))
            summed = lax.psum_scatter(
                total, "mp", scatter_dimension=0, axis_index_groups=same_core, tiled=True
            )
            return total, summed[0]

        results = []
        total, last, waiting = [], [], None
        for s in range(jobs + 1):
            if s < jobs:
                keep, gives, from_y = products(s, last + total)
                last = gives[:1]
            if waiting is not None:
                total, summed = over_z(*waiting, last, results[-1:])
                total = [total]
                results.append(summed)
            waiting = keep, from_y
        result = jnp.concatenate(results, -1)
        return result[0], result[1]

    return local


def solution(mesh):
    in_specs = (
        P("dp", "mp"),
        P("dp", "mp"),
        P("dp", "mp"),
        P("mp", "dp"),
        P(None, "mp"),
        P(None, "mp"),
        P("mp", None),
    )
    out_specs = (P("dp", "mp"), P("dp", "mp"))
    local = make_local(mesh.shape["dp"], mesh.shape["mp"])
    return jax.shard_map(local, mesh=mesh, in_specs=in_specs, out_specs=out_specs, check_vma=False)
```
